32 devices in a mesh: slab: 8 (over z, y), chan: 4 (over x, core).
Axes of the slice: x: 2, y: 2, z: 4, core: 2. Of those that a mesh axis runs over, the one named last changes fastest.
Arguments:
- volume: bfloat16 [2, 32, 128, 32, 128], P(None, 'slab', 'chan'), may hold values from -6 to 6
- first_kernel: bfloat16 [3, 3, 3, 128, 128], P(None, None, None, None, 'chan'), may hold values from -0.109375 to 0.109375
- first_bias: float32 [128], P('chan'), may hold values from -3 to 3
- second_kernel: bfloat16 [3, 3, 3, 128, 128], P(None, None, None, 'chan'), may hold values from -0.109375 to 0.109375
- second_bias: float32 [128], P('chan'), may hold values from -3 to 3
Outputs:
- features_out: bfloat16 [2, 32, 128, 32, 128], P(None, 'slab', 'chan')
The draws below stay inside these ranges and needn't reach their ends.
All inputs are finite; a program needn't handle non-finite values.
Results may differ from the reference program's by a relative error of at most 0.0046.
Values may be sent and summed in bfloat16 or wider, within the bound.
No kernel may reach another device: no remote copies, remote signals or barrier semaphores. Data moves between devices by JAX's collectives and lax.ppermute only.
A program may use at most 128 MiB of HBM per device.

```python
import jax
import jax.numpy as jnp
from jax import lax

C = 128
BATCH = 2
THICK = 32
NY = 128
DEPTH = 32


def levels(own_key, dims, pieces, smallest, high):
    gain = 1.0
    for axis_at, shards_of in pieces:
        draws = jax.random.uniform(jax.random.fold_in(jax.random.fold_in(own_key, 6), axis_at), (shards_of,), jnp.float32, smallest / len(pieces), high / len(pieces))
        gain = gain * jnp.repeat(jnp.exp(draws), dims[axis_at] // shards_of).reshape((-1,) + (1,) * (len(dims) - 1 - axis_at))
    return gain


def scatter_about(stream_key, extent, spread, reach, shards=(), held_as=jnp.bfloat16):
    values = spread * jax.random.normal(stream_key, extent, jnp.float32)
    if shards:
        values = values * levels(stream_key, extent, shards, -0.22, 0.18)
    return jnp.clip(values, -reach, reach).astype(held_as)


def setup_inputs(seed: int = 0) -> dict:
    streams_of = jax.random.split(jax.random.key(seed), 6)
    return {
        "volume": scatter_about(streams_of[0], (BATCH, DEPTH, C, THICK, NY), 1.0, 6.0, ((1, 8), (2, 4))),
        "first_kernel": scatter_about(streams_of[1], (3, 3, 3, C, C), (27 * C) ** -0.5, 0.109375, ((4, 4),)),
        "first_bias": scatter_about(streams_of[2], (C,), 0.5, 3.0, ((0, 4),), jnp.float32),
        "second_kernel": scatter_about(streams_of[3], (3, 3, 3, C, C), (27 * C) ** -0.5, 0.109375, ((3, 4),)),
        "second_bias": scatter_about(streams_of[4], (C,), 0.5, 3.0, ((0, 4),), jnp.float32),
    }


layout_spec = ("NDCHW", "DHWIO", "NDCHW")


def conv_layer(values_in, kernel, bias_row):
    summed = lax.conv_general_dilated(values_in.astype(jnp.float32), kernel.astype(jnp.float32), (1, 1, 1), ((1, 1), (1, 1), (1, 1)), dimension_numbers=layout_spec, precision=lax.Precision.HIGHEST)
    return jax.nn.relu(summed + bias_row.astype(jnp.float32)[None, None, :, None, None]).astype(jnp.bfloat16)


def reference(volume, first_kernel, first_bias, second_kernel, second_bias):
    hidden = conv_layer(volume, first_kernel, first_bias)
    return conv_layer(hidden, second_kernel, second_bias)
```

```python
import functools

import jax
import jax.numpy as jnp
from jax import lax
from jax.experimental import pallas as pl
from jax.experimental.pallas import tpu as pltpu
from jax.sharding import PartitionSpec as P

BF = jnp.bfloat16
VMEM_LIMIT = 48 * 2**20


def chan_swap(value, k):
    return lax.ppermute(value, "chan", [(i, i ^ k) for i in range(4)])


def slab_up(value):
    size = lax.axis_size("slab")
    return lax.ppermute(value, "slab", [(i, i + 1) for i in range(size - 1)])


def slab_down(value):
    size = lax.axis_size("slab")
    return lax.ppermute(value, "slab", [(i + 1, i) for i in range(size - 1)])


def rows(value, axis, start, count):
    return lax.dynamic_slice_in_dim(value, start, count, axis=axis)


def conv_rows(x, w, bias, depth, count, store):
    chans, width = x.shape[2], x.shape[3]
    lane = lax.broadcasted_iota(jnp.int32, (chans, width), 1)

    def step(j, _):
        for z in range(0, depth, 2):
            cols = [
                jnp.concatenate([x[z + u + a, j + c] for a in range(3) for c in range(3)], axis=0)
                for u in range(2)
            ]
            lhs = jnp.concatenate([w[k] for k in range(9)], axis=1)
            acc = jnp.dot(lhs, jnp.concatenate(cols, axis=1), preferred_element_type=jnp.float32)
            for u in range(2):
                part = acc[:, u * width : (u + 1) * width]
                before = jnp.where(lane == 0, 0.0, pltpu.roll(part[:chans], 1, 1))
                after = jnp.where(lane == width - 1, 0.0, pltpu.roll(part[2 * chans :], width - 1, 1))
                total = before + part[chans : 2 * chans] + after
                store(z + u, j, jnp.maximum(total + bias[...], 0.0).astype(BF))
        return 0

    lax.fori_loop(0, count, step, 0)


def run_copies(pairs, sems):
    copies = [pltpu.make_async_copy(s, d, sems.at[i]) for i, (s, d) in enumerate(pairs)]
    for copy in copies:
        copy.start()
    return copies


def first_kernel_body(chunk, count, own, *refs):
    if chunk == 0:
        new, old, w, bias = refs[:4], None, refs[4], refs[5]
        out_lo, out_mid, out_hi, x, sems = refs[6:]
    else:
        new, old, w, bias = refs[:4], refs[4:8], refs[8], refs[9]
        out_lo, out_mid, out_hi, x, sems = refs[10:]
    me = lax.axis_index("chan")
    b, c = me // 2, me % 2
    depth = own.shape[1]
    thick = own.shape[2]
    unit = own.shape[3]

    def pieces(four, have, own_at, x_at, skip, n, dst):
        xr, sr, lo, hi = four
        to = pl.ds(dst, n)
        inner = pl.ds(1, depth)
        out = [
            (own.at[b, :, pl.ds(own_at + skip, n)], x.at[inner, to, pl.ds(0, unit)]),
            (xr.at[:, pl.ds(x_at + skip, n)], x.at[inner, to, pl.ds(unit, unit)]),
        ]
        for k in range(2):
            out.append((sr.at[k, :, pl.ds(skip, n)], x.at[inner, to, pl.ds((2 + k) * unit, unit)]))
        for k in range(4):
            out.append((lo.at[k, pl.ds(skip, n)], x.at[0, to, pl.ds(k * unit, unit)]))
            out.append((hi.at[k, pl.ds(skip, n)], x.at[depth + 1, to, pl.ds(k * unit, unit)]))
        return out

    half = thick // 2
    n0 = half // 2 + 2
    if chunk == 0:
        pairs = pieces(new, n0, c * (thick - n0), c * n0, 0, n0, 1 - c)
        edge = jnp.where(c == 0, 0, n0)
    else:
        n1 = half // 2
        lead = n1 - 4
        pairs = pieces(new, n1, n0 + c * lead, c * lead, 0, n1, 2 - 2 * c)
        pairs += pieces(old, 2, c * (thick - n0), c * n0, (1 - c) * (n0 - 2), 2, c * n1)
        edge = None
    copies = run_copies(pairs, sems)
    if edge is not None:
        for z in range(depth + 2):
            x[z, edge] = jnp.zeros(x.shape[2:], BF)
    for copy in copies:
        copy.wait()

    def store(z, j, value):
        if z == 0:
            out_lo[j] = value
        elif z == depth - 1:
            out_hi[j] = value
        else:
            out_mid[z - 1, j] = value

    conv_rows(x, w, bias, depth, count, store)


def second_kernel_body(chunk, count, *refs):
    if chunk == 0:
        new, old, w, bias = refs[:5], None, refs[5], refs[6]
        outs, x, sems = refs[7:11], refs[11], refs[12]
    else:
        new, old, w, bias = refs[:5], refs[5:10], refs[10], refs[11]
        outs, x, sems = refs[12:16], refs[16], refs[17]
    c = lax.axis_index("chan") % 2
    depth = x.shape[0] - 2
    unit = outs[0].shape[2]

    def pieces(five, skip, n, dst):
        below, low, mid, high, above = five
        src, to = pl.ds(skip, n), pl.ds(dst, n)
        return [
            (below.at[src], x.at[0, to]),
            (low.at[src], x.at[1, to]),
            (mid.at[:, src], x.at[pl.ds(2, depth - 2), to]),
            (high.at[src], x.at[depth, to]),
            (above.at[src], x.at[depth + 1, to]),
        ]

    n0 = new[0].shape[0]
    if chunk == 0:
        pairs = pieces(new, 0, n0, 1 - c)
        edge = jnp.where(c == 0, 0, n0)
    else:
        h0 = old[0].shape[0]
        pairs = pieces(new, 0, n0, 2 - 2 * c)
        pairs += pieces(old, (1 - c) * (h0 - 2), 2, c * n0)
        edge = None
    copies = run_copies(pairs, sems)
    if edge is not None:
        for z in range(depth + 2):
            x[z, edge] = jnp.zeros(x.shape[2:], BF)
    for copy in copies:
        copy.wait()

    def store(z, j, value):
        for k in range(4):
            outs[k][z, j] = value[k * unit : (k + 1) * unit]

    conv_rows(x, w, bias, depth, count, store)


def call(body, count, depth, out_shapes, n_copies, chans, width, operands):
    any_spec = pl.BlockSpec(memory_space=pl.ANY)
    vmem = pl.BlockSpec(memory_space=pltpu.VMEM)
    flops = 2 * depth * count * width * 27 * chans * chans
    return pl.pallas_call(
        body,
        out_shape=[jax.ShapeDtypeStruct(s, BF) for s in out_shapes],
        in_specs=[any_spec] * (len(operands) - 2) + [vmem, vmem],
        out_specs=[vmem] * len(out_shapes),
        scratch_shapes=[
            pltpu.VMEM((depth + 2, count + 2, chans, width), BF),
            pltpu.SemaphoreType.DMA((n_copies,)),
        ],
        cost_estimate=pl.CostEstimate(flops=3 * flops, bytes_accessed=2**21, transcendentals=0),
        compiler_params=pltpu.CompilerParams(vmem_limit_bytes=VMEM_LIMIT),
    )(*operands)


def body(volume, first_kernel, first_bias, second_kernel, second_bias):
    _, depth, unit, thick, width = volume.shape
    chans = 4 * unit
    half = thick // 2
    n0, n1 = half // 2 + 2, half // 2
    lead = n1 - 4
    me = lax.axis_index("chan")
    b, c = me // 2, me % 2
    order = [me, me ^ 2, me ^ 1, me ^ 3]

    xt = jnp.transpose(volume, (0, 1, 3, 2, 4))
    away = lax.dynamic_index_in_dim(xt, 1 - b, 0, keepdims=False)
    home = lax.dynamic_index_in_dim(xt, b, 0, keepdims=False)
    xr0 = chan_swap(jnp.concatenate([away[:, :n0], away[:, thick - n0 :]], axis=1), 2)
    xr1 = chan_swap(away[:, n0 : thick - n0], 2)

    def reorder(value, axis):
        return jnp.concatenate([lax.dynamic_slice_in_dim(value, k * unit, unit, axis=axis) for k in order], axis=axis)

    w1 = jnp.transpose(reorder(first_kernel, 3), (0, 1, 2, 4, 3)).reshape(27, unit, chans)
    w2 = reorder(second_kernel, 4).reshape(27, unit, chans)
    mine = jnp.stack([w1, w2])
    pair = jnp.stack([mine, chan_swap(mine, 2)])
    four = jnp.concatenate([pair, chan_swap(pair, 1)])
    four = jnp.stack(
        [jnp.concatenate([four[m, ..., (j ^ m) * unit : ((j ^ m) + 1) * unit] for j in range(4)], axis=-1) for m in range(4)]
    )
    full1 = jnp.transpose(four[:, 0], (1, 0, 2, 3)).reshape(9, 3 * chans, chans)
    full2 = jnp.transpose(four[:, 1], (1, 3, 0, 2)).reshape(9, 3 * chans, chans)
    biases = jnp.stack([first_bias, second_bias])
    biases = jnp.concatenate([biases, chan_swap(biases, 2)], axis=1)
    spread = jnp.concatenate([biases, chan_swap(biases, 1)], axis=1)
    bias1 = jnp.broadcast_to(spread[0][:, None], (chans, width))
    bias2 = jnp.broadcast_to(spread[1][:, None], (chans, width))

    def gathered(xr, n, own_at, x_at):
        o = 1 - c
        sr = chan_swap(jnp.stack([rows(home, 1, own_at(o), n), rows(xr, 1, x_at(o), n)]), 1)
        mine_own, mine_x = rows(home, 1, own_at(c), n), rows(xr, 1, x_at(c), n)

        def layer(z):
            return jnp.concatenate([mine_own[z][None], mine_x[z][None], sr[:, z]])

        return xr, sr, slab_up(layer(depth - 1)), slab_down(layer(0))

    in0 = gathered(xr0, n0, lambda k: k * (thick - n0), lambda k: k * n0)
    in1 = gathered(xr1, n1, lambda k: n0 + k * lead, lambda k: k * lead)

    def hidden_shapes(n):
        return [(n, chans, width), (depth - 2, n, chans, width), (n, chans, width)]

    h0, h1 = n0 - 1, n1
    low0, mid0, high0 = call(
        functools.partial(first_kernel_body, 0, h0), h0, depth, hidden_shapes(h0), 12, chans, width,
        (xt, *in0, full1, bias1),
    )
    hid0 = (slab_up(high0), low0, mid0, high0, slab_down(low0))
    low1, mid1, high1 = call(
        functools.partial(first_kernel_body, 1, h1), h1, depth, hidden_shapes(h1), 24, chans, width,
        (xt, *in1, *in0, full1, bias1),
    )
    hid1 = (slab_up(high1), low1, mid1, high1, slab_down(low1))

    blocks = [(depth, n1, unit, width)] * 4
    got = []
    for chunk, hid in ((0, hid0), (1, hid1 + hid0)):
        outs = call(
            functools.partial(second_kernel_body, chunk, n1), n1, depth, blocks, 5 + 5 * chunk, chans, width,
            (*hid, full2, bias2),
        )
        got.append([outs[0], chan_swap(outs[1], 2), chan_swap(outs[2], 1), chan_swap(outs[3], 3)])

    def halves(first, second):
        as0 = jnp.concatenate([first[0], first[1], second[1], second[0]], axis=1)
        as1 = jnp.concatenate([second[0], second[1], first[1], first[0]], axis=1)
        return jnp.where(c == 0, as0, as1)

    at_home = halves([g[0] for g in got], [g[2] for g in got])
    abroad = halves([g[1] for g in got], [g[3] for g in got])
    out = jnp.where(b == 0, jnp.stack([at_home, abroad]), jnp.stack([abroad, at_home]))
    return jnp.transpose(out, (0, 1, 3, 2, 4))


def solution(mesh):
    return jax.shard_map(
        body,
        mesh=mesh,
        in_specs=(
            P(None, "slab", "chan", None, None),
            P(None, None, None, None, "chan"),
            P("chan"),
            P(None, None, None, "chan", None),
            P("chan"),
        ),
        out_specs=P(None, "slab", "chan", None, None),
        check_vma=False,
    )
```

```python
import functools

import jax
import jax.numpy as jnp
from jax import lax
from jax.experimental import pallas as pl
from jax.experimental.pallas import tpu as pltpu
from jax.sharding import PartitionSpec as P

BF = jnp.bfloat16
VMEM_LIMIT = 48 * 2**20
PARTS = 2


def chan_swap(value, k):
    return lax.ppermute(value, "chan", [(i, i ^ k) for i in range(4)])


def slab_swap(value, odd):
    size = lax.axis_size("slab")
    pairs = [(i, i + 1) for i in range(odd, size - 1, 2)]
    return lax.ppermute(value, "slab", pairs + [(j, i) for i, j in pairs])


def after(value, *earlier):
    return lax.optimization_barrier((value, earlier))[0]


def position():
    me = lax.axis_index("chan")
    return me, me // 2, me % 2, 1 - lax.axis_index("slab") % 2


def layer_at(r, depth, even):
    return jnp.where(even == 1, depth - 1 - r, r)


def conv_rows(x, w, bias, depth, count, even, store):
    chans, width = x.shape[2], x.shape[3]
    lane = lax.broadcasted_iota(jnp.int32, (chans, width), 1)

    def step(j, _):
        for r in range(0, depth, 2):
            cols = [
                jnp.concatenate(
                    [x[layer_at(r + u, depth, even) + a, j + c] for a in range(3) for c in range(3)], axis=0
                )
                for u in range(2)
            ]
            lhs = jnp.concatenate([w[3 * k : 3 * k + 3].reshape(3 * chans, chans) for k in range(9)], axis=1)
            acc = jnp.dot(lhs, jnp.concatenate(cols, axis=1), preferred_element_type=jnp.float32)
            for u in range(2):
                part = acc[:, u * width : (u + 1) * width]
                before = jnp.where(lane == 0, 0.0, pltpu.roll(part[:chans], 1, 1))
                later = jnp.where(lane == width - 1, 0.0, pltpu.roll(part[2 * chans :], width - 1, 1))
                total = before + part[chans : 2 * chans] + later
                store(r + u, j, jnp.maximum(total + bias[...], 0.0).astype(BF))
        return 0

    lax.fori_loop(0, count, step, 0)


def run_copies(pairs, sems, meanwhile):
    copies = [pltpu.make_async_copy(s, d, sems.at[i]) for i, (s, d) in enumerate(pairs)]
    for copy in copies:
        copy.start()
    meanwhile()
    for copy in copies:
        copy.wait()


def clear_edge(x, c, old):
    def clear():
        if not old:
            for z in range(x.shape[0]):
                x[z, jnp.where(c == 0, 0, x.shape[1] - 1)] = jnp.zeros(x.shape[2:], BF)

    return clear


def places(old, new, c):
    n = new[0].shape[1]
    if not old:
        return [(new, 0, n, 1 - c)]
    m = old[0].shape[1]
    return [(new, 0, n, 2 - 2 * c), (old, (1 - c) * (m - 2), 2, c * n)]


def first_kernel_body(count, has_old, *refs):
    new, refs = refs[:6], refs[6:]
    old, refs = (refs[:6], refs[6:]) if has_old else (None, refs)
    weights, bias, (out_a, out_mid, out_b, x, w, sems) = refs[:4], refs[4], refs[5:]
    me, _, c, even = position()
    depth, unit = new[0].shape[0], new[0].shape[2]
    pairs = []
    for k in range(4):
        pairs.append((weights[k].at[0], w.at[:, pl.ds(k * unit, unit)]))
    for arrays, start, n, dst in places(old, new, c):
        src, to = pl.ds(start, n), pl.ds(dst, n)
        for k in range(4):
            chan = pl.ds(pl.multiple_of((me ^ k) * unit, unit), unit)
            pairs.append((arrays[k].at[:, src], x.at[pl.ds(1, depth), to, chan]))
            pairs.append((arrays[4].at[k, src], x.at[1 + layer_at(-1, depth, even), to, chan]))
            pairs.append((arrays[5].at[k, src], x.at[1 + layer_at(depth, depth, even), to, chan]))
    run_copies(pairs, sems, clear_edge(x, c, old))

    def store(r, j, value):
        if r == 0:
            out_a[0, j] = value
        elif r == depth - 1:
            out_b[0, j] = value
        else:
            out_mid[r - 1, j] = value

    conv_rows(x, w, bias, depth, count, even, store)


def second_kernel_body(count, has_old, *refs):
    new, refs = refs[:5], refs[5:]
    old, refs = (refs[:5], refs[5:]) if has_old else (None, refs)
    w, bias, outs, (x, sems) = refs[0], refs[1], refs[2:6], refs[6:]
    _, _, c, even = position()
    depth, unit = x.shape[0] - 2, outs[0].shape[2]
    pairs = []
    for arrays, start, n, dst in places(old, new, c):
        src, to = pl.ds(start, n), pl.ds(dst, n)
        r = -1
        for part in arrays:
            for k in range(part.shape[0]):
                pairs.append((part.at[k, src], x.at[1 + layer_at(r, depth, even), to]))
                r += 1
    run_copies(pairs, sems, clear_edge(x, c, old))

    def store(r, j, value):
        for k in range(4):
            outs[k][layer_at(r, depth, even), j] = value[k * unit : (k + 1) * unit]

    conv_rows(x, w, bias, depth, count, even, store)


def weights_kernel_body(*refs):
    pieces, (out, w, sems) = refs[:4], refs[4:]
    me = lax.axis_index("chan")
    unit = pieces[0].shape[2]
    run_copies([(pieces[k].at[1], w.at[:, pl.ds(k * unit, unit)]) for k in range(4)], sems, lambda: None)

    def step(i, _):
        turned = jnp.transpose(w[i])
        for q in range(4):
            out[i, pl.ds(pl.multiple_of((me ^ q) * unit, unit), unit)] = turned[q * unit : (q + 1) * unit]
        return 0

    lax.fori_loop(0, w.shape[0], step, 0, unroll=3)


def call(body, outs, any_operands, vmem_operands, scratch, n_copies, flops):
    any_spec = pl.BlockSpec(memory_space=pl.ANY)
    vmem = pl.BlockSpec(memory_space=pltpu.VMEM)
    return pl.pallas_call(
        body,
        out_shape=[jax.ShapeDtypeStruct(s, BF) for s in outs],
        in_specs=[any_spec] * len(any_operands) + [vmem] * len(vmem_operands),
        out_specs=[vmem] * len(outs),
        scratch_shapes=[*(pltpu.VMEM(s, BF) for s in scratch), pltpu.SemaphoreType.DMA((n_copies,))],
        cost_estimate=pl.CostEstimate(flops=flops, bytes_accessed=2**21, transcendentals=0),
        compiler_params=pltpu.CompilerParams(vmem_limit_bytes=VMEM_LIMIT),
    )(*any_operands, *vmem_operands)


def body(volume, first_kernel, first_bias, second_kernel, second_bias):
    _, depth, unit, thick, width = volume.shape
    chans = 4 * unit
    half = thick // 2
    _, b, c, even = position()
    ends = [half * k // PARTS for k in range(PARTS + 1)]
    in_ends = [0] + [e + 2 for e in ends[1:]]
    hidden_ends = [0] + [e + 1 for e in ends[1:]]

    def cut(chunk, k):
        first, last = in_ends[chunk], in_ends[chunk + 1]
        start = jnp.where(c ^ (k & 1) == 0, first, thick - last)
        zero = jnp.int32(0)
        part = lax.dynamic_slice(
            volume, (b ^ (k >> 1), zero, zero, start, zero), (1, depth, unit, last - first, width)
        )
        return jnp.transpose(part[0], (0, 2, 1, 3))

    def outer(value, r):
        return lax.dynamic_index_in_dim(value, layer_at(r, depth, even), 0, keepdims=False)

    received = []
    got = None
    weights = None
    for chunk in range(PARTS):
        sent = [cut(chunk, k) for k in (2, 3, 1)]
        if got is not None:
            sent = after(sent, got)
        got = [chan_swap(v, k) for v, k in zip(sent, (2, 3, 1))]
        v = [cut(chunk, 0), got[2], got[0], got[1]]
        side = [slab_swap(jnp.stack([outer(p, r) for p in v]), odd) for odd, r in ((0, 0), (1, depth - 1))]
        received.append((*v, *side))
        if chunk == 0:
            w1 = jnp.transpose(first_kernel, (0, 1, 2, 4, 3)).reshape(27, unit, chans)
            mine = jnp.stack([w1, second_kernel.reshape(27, unit, chans)])
            across = chan_swap(after(mine, got), 2)
            weights = (mine, chan_swap(mine, 1), across, chan_swap(across, 1))

    biases = jnp.stack([first_bias, second_bias])
    biases = jnp.concatenate([biases, chan_swap(biases, 1)], axis=1)
    biases = jnp.concatenate([biases, chan_swap(biases, 2)], axis=1)
    bias1, bias2 = (jnp.broadcast_to(v[:, None], (chans, width)) for v in biases)
    full2 = call(weights_kernel_body, [(27, chans, chans)], weights, (), [(27, chans, chans)], 4, 10**9)[0]

    unit_flops = 3 * 2 * depth * width * 27 * chans * chans
    hidden = []
    for chunk in range(PARTS):
        n = hidden_ends[chunk + 1] - hidden_ends[chunk]
        operands = received[chunk] + (received[chunk - 1] if chunk else ())
        edge_a, mid, edge_b = call(
            functools.partial(first_kernel_body, n, chunk > 0),
            [(1, n, chans, width), (depth - 2, n, chans, width), (1, n, chans, width)],
            (*operands, *weights), (bias1,),
            [(depth + 2, n + 2, chans, width), (27, chans, chans)],
            4 + 12 * (1 + (chunk > 0)), unit_flops * n,
        )
        hidden.append((slab_swap(edge_a, 0), edge_a, mid, edge_b, slab_swap(edge_b, 1)))

    done = []
    for chunk in range(PARTS):
        n = ends[chunk + 1] - ends[chunk]
        operands = hidden[chunk] + (hidden[chunk - 1] if chunk else ())
        outs = call(
            functools.partial(second_kernel_body, n, chunk > 0),
            [(depth, n, unit, width)] * 4,
            operands, (full2, bias2),
            [(depth + 2, n + 2, chans, width)],
            (depth + 2) * (1 + (chunk > 0)), unit_flops * n,
        )
        done.append([outs[0], *(chan_swap(outs[k], k) for k in (1, 2, 3))])

    def halves(near, far):
        lower = jnp.concatenate(near + far[::-1], axis=1)
        upper = jnp.concatenate(far + near[::-1], axis=1)
        return jnp.where(c == 0, lower, upper)

    home = halves([d[0] for d in done], [d[1] for d in done])
    away = halves([d[2] for d in done], [d[3] for d in done])
    out = jnp.where(b == 0, jnp.stack([home, away]), jnp.stack([away, home]))
    return jnp.transpose(out, (0, 1, 3, 2, 4))


def solution(mesh):
    return jax.shard_map(
        body,
        mesh=mesh,
        in_specs=(
            P(None, "slab", "chan", None, None),
            P(None, None, None, None, "chan"),
            P("chan"),
            P(None, None, None, "chan", None),
            P("chan"),
        ),
        out_specs=P(None, "slab", "chan", None, None),
        check_vma=False,
    )
```

```python
import functools

import jax
import jax.numpy as jnp
from jax import lax
from jax.experimental import pallas as pl
from jax.experimental.pallas import tpu as pltpu
from jax.sharding import PartitionSpec as P

BF = jnp.bfloat16
VMEM_LIMIT = 48 * 2**20
CUTS = (9, 21, 32)
UNROLL = 3


def chan_swap(value, k):
    return lax.ppermute(value, "chan", [(i, i ^ k) for i in range(4)])


def slab_swap(value):
    size = lax.axis_size("slab")
    pairs = [(4 * s + i + 1, 4 * (s + 1) + i) for s in range(size - 1) for i in (0, 2)]
    return lax.ppermute(value, ("slab", "chan"), pairs + [(j, i) for i, j in pairs])


def after(value, *earlier):
    return lax.optimization_barrier((value, earlier))[0]


def conv_rows(x, w, bias, first, second, count, store):
    chans, width = x.shape[2], x.shape[3]
    lane = lax.broadcasted_iota(jnp.int32, (chans, width), 1)

    def step(j, _):
        cols = [
            jnp.concatenate([x[z + a, j + c] for a in range(3) for c in range(3)], axis=0) for z in (first, second)
        ]
        lhs = jnp.concatenate([w[3 * k : 3 * k + 3].reshape(3 * chans, chans) for k in range(9)], axis=1)
        acc = jnp.dot(lhs, jnp.concatenate(cols, axis=1), preferred_element_type=jnp.float32)
        for u in range(2):
            part = acc[:, u * width : (u + 1) * width]
            before = jnp.where(lane == 0, 0.0, pltpu.roll(part[:chans], 1, 1))
            later = jnp.where(lane == width - 1, 0.0, pltpu.roll(part[2 * chans :], width - 1, 1))
            total = before + part[chans : 2 * chans] + later
            store(u, j, jnp.maximum(total + bias[...], 0.0).astype(BF))
        return 0

    lax.fori_loop(0, count, step, 0, unroll=UNROLL)


def start_copies(pairs, sems, first=0):
    copies = [pltpu.make_async_copy(s, d, sems.at[first + i]) for i, (s, d) in enumerate(pairs)]
    for copy in copies:
        copy.start()
    return copies


def place(block, unit):
    return pl.ds(pl.multiple_of(block * unit, unit), unit)


def spans(new, old, axis):
    n = new[0].shape[axis]
    if old is None:
        return [(new, 0, n, 1)]
    return [(new, 0, n, 2), (old, old[0].shape[axis] - 2, 2, 0)]


def clear_edges(x, has_old, last):
    edges = ([] if has_old else [0]) + ([x.shape[1] - 1] if last else [])
    for row in edges:
        for z in range(x.shape[0]):
            x[z, row] = jnp.zeros(x.shape[2:], BF)


def first_kernel_body(has_old, last, *refs):
    new, refs = refs[:4], refs[4:]
    old, refs = (refs[:4], refs[4:]) if has_old else (None, refs)
    (w_own, w_x, w_s), bias, (out_slab, out_sib, x, w, sems) = refs[:3], refs[3], refs[4:]
    me = lax.axis_index("chan")
    c = me % 2
    unit = w_own.shape[1]
    pairs = [
        (block, w.at[:, place(me ^ k, unit)]) for k, block in enumerate((w_own, w_s.at[0], w_x, w_s.at[1]))
    ]
    for (own, xr, sr, side), start, rows, dst in spans(new, old, 1):
        src, to = pl.ds(start, rows), pl.ds(dst, rows)
        three = pl.ds(c, 3)
        for k, block in enumerate((own.at[three, src], sr.at[0, :, src], xr.at[three, src], sr.at[1, :, src])):
            pairs.append((block, x.at[pl.ds(1 - c, 3), to, place(me ^ k, unit)]))
            pairs.append((side.at[k, src], x.at[3 * c, to, place(me ^ 1 ^ k, unit)]))
    copies = start_copies(pairs, sems)
    clear_edges(x, has_old, last)
    for copy in copies:
        copy.wait()

    def store(u, j, value):
        (out_slab, out_sib)[u][j] = value

    conv_rows(x, w, bias, c, 1 - c, out_slab.shape[0], store)


def second_kernel_body(has_old, last, *refs):
    new, refs = refs[:4], refs[4:]
    old, refs = (refs[:4], refs[4:]) if has_old else (None, refs)
    w, bias, outs, (h, sems) = refs[0], refs[1], refs[2:-2], refs[-2:]
    if len(outs) == 3:
        outs = (outs[0], outs[1], outs[2].at[0], outs[2].at[1])
    c = lax.axis_index("chan") % 2
    unit = outs[0].shape[2]
    pairs = []
    for arrays, start, rows, dst in spans(new, old, 0):
        for part, z in zip(arrays, (3 * c, 1 + c, 2 - c, 3 - 3 * c)):
            pairs.append((part.at[pl.ds(start, rows)], h.at[z, pl.ds(dst, rows)]))
    copies = start_copies(pairs, sems)
    clear_edges(h, has_old, last)
    for copy in copies:
        copy.wait()

    def store(u, j, value):
        for k in range(4):
            outs[k][u, j] = value[k * unit : (k + 1) * unit]

    conv_rows(h, w, bias, 0, 1, outs[0].shape[1], store)


def weights_kernel_body(*refs):
    (own, across, shared), (out, w, sems) = refs[:3], refs[3:]
    pieces = (own, shared.at[0], across, shared.at[1])
    me = lax.axis_index("chan")
    unit = own.shape[1]
    for copy in start_copies([(pieces[k], w.at[:, place(me ^ k, unit)]) for k in range(4)], sems):
        copy.wait()

    def step(i, _):
        turned = jnp.transpose(w[i])
        for q in range(4):
            out[i, place(me ^ q, unit)] = turned[q * unit : (q + 1) * unit]
        return 0

    lax.fori_loop(0, w.shape[0], step, 0, unroll=3)


def call(body, outs, any_operands, vmem_operands, scratch, n_copies, flops):
    any_spec = pl.BlockSpec(memory_space=pl.ANY)
    vmem = pl.BlockSpec(memory_space=pltpu.VMEM)
    return pl.pallas_call(
        body,
        out_shape=[jax.ShapeDtypeStruct(s, BF) for s in outs],
        in_specs=[any_spec] * len(any_operands) + [vmem] * len(vmem_operands),
        out_specs=[vmem] * len(outs),
        scratch_shapes=[*(pltpu.VMEM(s, BF) for s in scratch), pltpu.SemaphoreType.DMA((n_copies,))],
        cost_estimate=pl.CostEstimate(flops=flops, bytes_accessed=2**21, transcendentals=0),
        compiler_params=pltpu.CompilerParams(vmem_limit_bytes=VMEM_LIMIT),
    )(*any_operands, *vmem_operands)


def body(volume, first_kernel, first_bias, second_kernel, second_bias):
    _, depth, unit, thick, width = volume.shape
    chans = 4 * unit
    me = lax.axis_index("chan")
    b, c = me // 2, me % 2
    ends = [0] + [thick * k // CUTS[-1] for k in CUTS]
    parts = len(CUTS)
    in_ends = [0] + [e + 2 for e in ends[1:-1]] + [thick]
    hidden_ends = [0] + [e + 1 for e in ends[1:-1]] + [thick]

    def cut(chunk, batch):
        part = lax.dynamic_index_in_dim(volume, batch, 0, keepdims=False)
        return jnp.transpose(part[:, :, in_ends[chunk] : in_ends[chunk + 1]], (0, 2, 1, 3))

    def layer(value, z):
        return lax.dynamic_index_in_dim(value, z, 0, keepdims=False)

    def share(own, xr):
        three = [lax.dynamic_slice_in_dim(v, 1 - c, 3) for v in (own, xr)]
        sr = chan_swap(jnp.stack(three), 1)
        edge = jnp.stack([layer(own, 3 * c), layer(sr[0], 2 * c), layer(xr, 3 * c), layer(sr[1], 2 * c)])
        return (own, xr, sr, slab_swap(edge)), edge

    def weight_pieces(own, earlier):
        across = chan_swap(after(own, earlier), 2)
        return (own, across, chan_swap(jnp.stack([own, across]), 1))

    sent = cut(0, 1 - b)
    xr = chan_swap(sent, 2)
    (volume, w1, w2, biases), _ = lax.optimization_barrier(
        ((volume, first_kernel, second_kernel, (first_bias, second_bias)), sent)
    )
    biases = jnp.stack(biases)
    biases = jnp.concatenate([biases, chan_swap(biases, 1)], axis=1)
    biases = jnp.concatenate([biases, chan_swap(biases, 2)], axis=1)
    w1 = jnp.transpose(w1, (0, 1, 2, 4, 3)).reshape(27, unit, chans)
    w2 = w2.reshape(27, unit, chans)
    xr, biases = lax.optimization_barrier((xr, biases))
    received, edges = [], []
    for chunk in range(parts):
        arrays, edge = share(cut(chunk, b), xr)
        received.append(arrays)
        edges.append(edge)
        if chunk == 0:
            first = weight_pieces(w1, edge)
        if chunk < parts - 1:
            xr = chan_swap(after(cut(chunk + 1, 1 - b), xr, edge), 2)
    second = weight_pieces(w2, xr)

    order = [jnp.concatenate([layer(v.reshape(4, unit), me ^ q) for q in range(4)]) for v in biases[:1]] + [biases[1]]
    bias1, bias2 = (jnp.broadcast_to(v[:, None], (chans, width)) for v in order)
    full2 = call(weights_kernel_body, [(27, chans, chans)], second, (), [(27, chans, chans)], 4, 10**9)[0]

    unit_flops = 2 * 4 * width * 27 * chans * chans
    hidden = []
    for chunk in range(parts):
        n = hidden_ends[chunk + 1] - hidden_ends[chunk]
        operands = received[chunk] + (received[chunk - 1] if chunk else ())
        operands = after(operands, edges[chunk + 1 : chunk + 2])
        to_slab, to_sib = call(
            functools.partial(first_kernel_body, chunk > 0, chunk == parts - 1),
            [(n, chans, width)] * 2, (*operands, *first), (bias1,),
            [(4, n + 2, chans, width), (27, chans, chans)],
            4 + 8 * (1 + (chunk > 0)), unit_flops * n,
        )
        hidden.append((slab_swap(to_slab), to_slab, to_sib, chan_swap(to_sib, 1)))

    own, other, sibling, diagonal = [], [], [], []
    for chunk in range(parts):
        n = ends[chunk + 1] - ends[chunk]
        operands = hidden[chunk] + (hidden[chunk - 1] if chunk else ())
        operands = after(operands, [h[1] for h in hidden[chunk + 1 : chunk + 2]])
        last = chunk == parts - 1
        block = (2, n, unit, width)
        outs = call(
            functools.partial(second_kernel_body, chunk > 0, last),
            [block] * 4 if last else [block, block, (2, *block)], operands, (full2, bias2),
            [(4, n + 2, chans, width)], 4 * (1 + (chunk > 0)), unit_flops * n,
        )
        own.append(outs[0])
        if last:
            x, s, d = (chan_swap(outs[k], k) for k in (2, 1, 3))
        else:
            got = chan_swap(outs[2], 2)
            x = got[0]
            s, d = chan_swap(jnp.stack([outs[1], got[1]]), 1)
        other.append(x)
        sibling.append(s)
        diagonal.append(d)

    def layers(near, far):
        near, far = jnp.concatenate(near, axis=1), jnp.concatenate(far, axis=1)
        return jnp.where(c == 0, jnp.concatenate([near, far]), jnp.concatenate([far, near]))

    home = layers(own, sibling)
    away = layers(other, diagonal)
    out = jnp.where(b == 0, jnp.stack([home, away]), jnp.stack([away, home]))
    return jnp.transpose(out, (0, 1, 3, 2, 4))


def solution(mesh):
    return jax.shard_map(
        body,
        mesh=mesh,
        in_specs=(
            P(None, "slab", "chan", None, None),
            P(None, None, None, None, "chan"),
            P("chan"),
            P(None, None, None, "chan", None),
            P("chan"),
        ),
        out_specs=P(None, "slab", "chan", None, None),
        check_vma=False,
    )
```

```python
import functools

import jax
import jax.numpy as jnp
from jax import lax
from jax.experimental import pallas as pl
from jax.experimental.pallas import tpu as pltpu
from jax.sharding import PartitionSpec as P

BF = jnp.bfloat16
VMEM_LIMIT = 48 * 2**20
CUTS = (11, 23, 32)
UNROLL = 3


def chan_swap(value, k):
    return lax.ppermute(value, "chan", [(i, i ^ k) for i in range(4)])


def slab_swap(value):
    size = lax.axis_size("slab")
    pairs = [(4 * s + i + 1, 4 * (s + 1) + i) for s in range(size - 1) for i in (0, 2)]
    return lax.ppermute(value, ("slab", "chan"), pairs + [(j, i) for i, j in pairs])


def after(value, *earlier):
    return lax.optimization_barrier((value, earlier))[0]


def conv_rows(x, w, bias, first, second, count, store):
    chans, width = x.shape[2], x.shape[3]
    lane = lax.broadcasted_iota(jnp.int32, (chans, width), 1)

    def step(j, _):
        cols = [
            jnp.concatenate([x[z + a, j + c] for a in range(3) for c in range(3)], axis=0) for z in (first, second)
        ]
        lhs = jnp.concatenate([w[3 * k : 3 * k + 3].reshape(3 * chans, chans) for k in range(9)], axis=1)
        acc = jnp.dot(lhs, jnp.concatenate(cols, axis=1), preferred_element_type=jnp.float32)
        for u in range(2):
            part = acc[:, u * width : (u + 1) * width]
            before = jnp.where(lane == 0, 0.0, pltpu.roll(part[:chans], 1, 1))
            later = jnp.where(lane == width - 1, 0.0, pltpu.roll(part[2 * chans :], width - 1, 1))
            total = before + part[chans : 2 * chans] + later
            store(u, j, jnp.maximum(total + bias[...], 0.0).astype(BF))
        return 0

    lax.fori_loop(0, count, step, 0, unroll=UNROLL)


def start_copies(pairs, sems, first=0):
    copies = [pltpu.make_async_copy(s, d, sems.at[first + i]) for i, (s, d) in enumerate(pairs)]
    for copy in copies:
        copy.start()
    return copies


def place(block, unit):
    return pl.ds(pl.multiple_of(block * unit, unit), unit)


def spans(new, old, axis):
    n = new[0].shape[axis]
    if old is None:
        return [(new, 0, n, 1)]
    return [(new, 0, n, 2), (old, old[0].shape[axis] - 2, 2, 0)]


def clear_edges(x, has_old, last):
    edges = ([] if has_old else [0]) + ([x.shape[1] - 1] if last else [])
    for row in edges:
        for z in range(x.shape[0]):
            x[z, row] = jnp.zeros(x.shape[2:], BF)


def first_kernel_body(has_old, last, *refs):
    new, refs = refs[:4], refs[4:]
    old, refs = (refs[:4], refs[4:]) if has_old else (None, refs)
    (w_own, w_x, w_s), bias, (out_slab, out_sib, x, w, sems) = refs[:3], refs[3], refs[4:]
    me = lax.axis_index("chan")
    c = me % 2
    unit = w_own.shape[1]
    pairs = [
        (block, w.at[:, place(me ^ k, unit)]) for k, block in enumerate((w_own, w_s.at[0], w_x, w_s.at[1]))
    ]
    for (own, xr, sr, side), start, rows, dst in spans(new, old, 1):
        src, to = pl.ds(start, rows), pl.ds(dst, rows)
        three = pl.ds(c, 3)
        for k, block in enumerate((own.at[three, src], sr.at[0, :, src], xr.at[three, src], sr.at[1, :, src])):
            pairs.append((block, x.at[pl.ds(1 - c, 3), to, place(me ^ k, unit)]))
            pairs.append((side.at[k, src], x.at[3 * c, to, place(me ^ 1 ^ k, unit)]))
    copies = start_copies(pairs, sems)
    clear_edges(x, has_old, last)
    for copy in copies:
        copy.wait()

    def store(u, j, value):
        (out_slab, out_sib)[u][j] = value

    conv_rows(x, w, bias, c, 1 - c, out_slab.shape[0], store)


def second_kernel_body(has_old, last, *refs):
    new, refs = refs[:4], refs[4:]
    old, refs = (refs[:4], refs[4:]) if has_old else (None, refs)
    w, bias, outs, (h, sems) = refs[0], refs[1], refs[2:-2], refs[-2:]
    if len(outs) == 3:
        outs = (outs[0], outs[1], outs[2].at[0], outs[2].at[1])
    c = lax.axis_index("chan") % 2
    unit = outs[0].shape[2]
    pairs = []
    for arrays, start, rows, dst in spans(new, old, 0):
        for part, z in zip(arrays, (3 * c, 1 + c, 2 - c, 3 - 3 * c)):
            pairs.append((part.at[pl.ds(start, rows)], h.at[z, pl.ds(dst, rows)]))
    copies = start_copies(pairs, sems)
    clear_edges(h, has_old, last)
    for copy in copies:
        copy.wait()

    def store(u, j, value):
        for k in range(4):
            outs[k][u, j] = value[k * unit : (k + 1) * unit]

    conv_rows(h, w, bias, 0, 1, outs[0].shape[1], store)


def weights_kernel_body(*refs):
    (own, across, shared), (out, w, sems) = refs[:3], refs[3:]
    pieces = (own, shared.at[0], across, shared.at[1])
    me = lax.axis_index("chan")
    unit = own.shape[1]
    for copy in start_copies([(pieces[k], w.at[:, place(me ^ k, unit)]) for k in range(4)], sems):
        copy.wait()

    def step(i, _):
        turned = jnp.transpose(w[i])
        for q in range(4):
            out[i, place(me ^ q, unit)] = turned[q * unit : (q + 1) * unit]
        return 0

    lax.fori_loop(0, w.shape[0], step, 0, unroll=3)


def call(body, outs, any_operands, vmem_operands, scratch, n_copies, flops):
    any_spec = pl.BlockSpec(memory_space=pl.ANY)
    vmem = pl.BlockSpec(memory_space=pltpu.VMEM)
    return pl.pallas_call(
        body,
        out_shape=[jax.ShapeDtypeStruct(s, BF) for s in outs],
        in_specs=[any_spec] * len(any_operands) + [vmem] * len(vmem_operands),
        out_specs=[vmem] * len(outs),
        scratch_shapes=[*(pltpu.VMEM(s, BF) for s in scratch), pltpu.SemaphoreType.DMA((n_copies,))],
        cost_estimate=pl.CostEstimate(flops=flops, bytes_accessed=2**21, transcendentals=0),
        compiler_params=pltpu.CompilerParams(vmem_limit_bytes=VMEM_LIMIT),
    )(*any_operands, *vmem_operands)


def body(volume, first_kernel, first_bias, second_kernel, second_bias):
    _, depth, unit, thick, width = volume.shape
    chans = 4 * unit
    me = lax.axis_index("chan")
    b, c = me // 2, me % 2
    ends = [0] + [thick * k // CUTS[-1] for k in CUTS]
    parts = len(CUTS)
    in_ends = [0] + [e + 2 for e in ends[1:-1]] + [thick]
    hidden_ends = [0] + [e + 1 for e in ends[1:-1]] + [thick]

    def cut(chunk, batch):
        part = lax.dynamic_index_in_dim(volume, batch, 0, keepdims=False)
        return jnp.transpose(part[:, :, in_ends[chunk] : in_ends[chunk + 1]], (0, 2, 1, 3))

    def layer(value, z):
        return lax.dynamic_index_in_dim(value, z, 0, keepdims=False)

    def share(own, xr):
        three = [lax.dynamic_slice_in_dim(v, 1 - c, 3) for v in (own, xr)]
        sr = chan_swap(jnp.stack(three), 1)
        edge = jnp.stack([layer(own, 3 * c), layer(sr[0], 2 * c), layer(xr, 3 * c), layer(sr[1], 2 * c)])
        return (own, xr, sr, slab_swap(edge)), edge

    sent = cut(0, 1 - b)
    xr = chan_swap(sent, 2)
    (volume, w1, w2, biases), _ = lax.optimization_barrier(
        ((volume, first_kernel, second_kernel, (first_bias, second_bias)), sent)
    )
    biases = jnp.stack(biases)
    biases = jnp.concatenate([biases, chan_swap(biases, 1)], axis=1)
    biases = jnp.concatenate([biases, chan_swap(biases, 2)], axis=1)
    w1 = jnp.transpose(w1, (0, 1, 2, 4, 3)).reshape(27, unit, chans)
    w2 = w2.reshape(27, unit, chans)
    home = [cut(k, b) for k in range(parts)]
    away = [None] + [cut(k, 1 - b) for k in range(1, parts)]
    xr, biases, w1, home[0], away[1] = lax.optimization_barrier((xr, biases, w1, home[0], away[1]))

    order = [jnp.concatenate([layer(v.reshape(4, unit), me ^ q) for q in range(4)]) for v in biases[:1]] + [biases[1]]
    bias1, bias2 = (jnp.broadcast_to(v[:, None], (chans, width)) for v in order)

    unit_flops = 4 * width * 27 * chans * chans
    received, hidden, weights = [], [], []

    def first_conv(chunk, edge):
        n = hidden_ends[chunk + 1] - hidden_ends[chunk]
        operands = received[chunk] + (received[chunk - 1] if chunk else ())
        if edge is not None:
            operands = after(operands, edge)
        to_slab, to_sib = call(
            functools.partial(first_kernel_body, chunk > 0, chunk == parts - 1),
            [(n, chans, width)] * 2, (*operands, *weights[0]), (bias1,),
            [(4, n + 2, chans, width), (27, chans, chans)],
            4 + 8 * (1 + (chunk > 0)), 2 * unit_flops * n,
        )
        hidden.append((slab_swap(to_slab), to_slab, to_sib, chan_swap(to_sib, 1)))
        return to_slab

    for chunk in range(parts):
        arrays, edge = share(home[chunk], xr)
        side = arrays[3]
        ready = []
        if chunk == 0:
            ready = [home[1:], away[2:], w2, bias1, bias2]
        else:
            ready = first_conv(chunk - 1, edge)
        before = xr
        if chunk < parts - 1:
            xr = chan_swap(after(away[chunk + 1], before), 2)
        if chunk < 2:
            own = (w1, w2)[chunk]
            across = chan_swap(after(own, before), 2)
            (side, xr, across), ready = lax.optimization_barrier(((side, xr, across), ready))
            weights.append((own, across, chan_swap(jnp.stack([own, across]), 1)))
        else:
            side, ready = lax.optimization_barrier((side, ready))
        if chunk == 0:
            home[1:], away[2:], w2, bias1, bias2 = ready
        received.append((*arrays[:3], side))
    first_conv(parts - 1, None)
    full2 = call(weights_kernel_body, [(27, chans, chans)], weights[1], (), [(27, chans, chans)], 4, 10**9)[0]

    own, other, sibling, diagonal = [], [], [], []
    for chunk in range(parts):
        n = ends[chunk + 1] - ends[chunk]
        operands = hidden[chunk] + (hidden[chunk - 1] if chunk else ())
        operands = after(operands, [h[1] for h in hidden[chunk + 1 : chunk + 2]])
        last = chunk == parts - 1
        if last:
            operands = after(operands, sibling[:-1])
        block = (2, n, unit, width)
        outs = call(
            functools.partial(second_kernel_body, chunk > 0, last),
            [block] * 4 if last else [block, block, (2, *block)], operands, (full2, bias2),
            [(4, n + 2, chans, width)], 4 * (1 + (chunk > 0)), 2 * unit_flops * n,
        )
        own.append(outs[0])
        if last:
            x, s, d = (chan_swap(outs[k], k) for k in (2, 1, 3))
        else:
            got = chan_swap(outs[2], 2)
            x, passed = got[0], jnp.stack([outs[1], got[1]])
            s, d = (None, None) if chunk == parts - 2 else chan_swap(passed, 1)
        other.append(x)
        sibling.append(s)
        diagonal.append(d)
    sibling[-2], diagonal[-2] = chan_swap(after(passed, sibling[-1]), 1)

    def layers(near, far):
        near, far = jnp.concatenate(near, axis=1), jnp.concatenate(far, axis=1)
        return jnp.where(c == 0, jnp.concatenate([near, far]), jnp.concatenate([far, near]))

    near, far = layers(own, sibling), layers(other, diagonal)
    out = jnp.where(b == 0, jnp.stack([near, far]), jnp.stack([far, near]))
    return jnp.transpose(out, (0, 1, 3, 2, 4))


def solution(mesh):
    return jax.shard_map(
        body,
        mesh=mesh,
        in_specs=(
            P(None, "slab", "chan", None, None),
            P(None, None, None, None, "chan"),
            P("chan"),
            P(None, None, None, "chan", None),
            P("chan"),
        ),
        out_specs=P(None, "slab", "chan", None, None),
        check_vma=False,
    )
```
